768 devices in a mesh: dp: 128 (over z_hi, y, x), tensor: 6 (over z_lo, core).
Axes of the slice: x: 4, y: 8, z: 12 (z_hi: 4, z_lo: 3; z = z_hi * 3 + z_lo), core: 2. Of those that a mesh axis runs over, the one named last changes fastest.
Arguments:
- grad: bfloat16 [4096, 12288], P('dp', 'tensor'), may hold values from -48 to 48
- second_moment: float32 [4096, 12288], P('dp', 'tensor'), may hold values from 0.05 to 5
- left_roots: bfloat16 [4, 1024, 1024], P(None, 'dp'), may hold values from -5 to 5
- right_roots: bfloat16 [12, 1024, 1024], P('tensor'), may hold values from -5 to 5
Outputs:
- update: bfloat16 [4096, 12288], P('dp', 'tensor')
- moment_next: float32 [4096, 12288], P('dp', 'tensor')
The draws below stay inside these ranges and needn't reach their ends.
All inputs are finite; a program needn't handle non-finite values.
Results may differ from the reference program's by a relative error of at most 0.0059.
Values may be sent and summed in bfloat16 or wider, within the bound.
No kernel may reach another device: no remote copies, remote signals or barrier semaphores. Data moves between devices by JAX's collectives and lax.ppermute only.
A program may use at most 32 MiB of HBM per device.

```python
import math
import jax
import jax.numpy as jnp
from jax import lax

DW = 4096
FFW = 12288
BLK = 1024
RBLK = 4
CBLK = 12


def draw_grad(key, part):
    key = jax.random.fold_in(key, 11)
    keys = jax.random.split(key, 3)
    base = jnp.clip(jax.random.normal(keys[0], (DW, FFW), jnp.float32), -4.0, 4.0)
    spread = 1.4
    rising = 3.0 ** (jnp.arange(DW, dtype=jnp.float32) / (DW - 1))
    row_scale = rising * jnp.exp(jax.random.uniform(keys[1], (DW,), jnp.float32, -jnp.log(spread), jnp.log(spread)))
    col_scale = jnp.exp(jax.random.uniform(keys[2], (FFW,), jnp.float32, -jnp.log(2.0), jnp.log(2.0)))
    return (base * row_scale[:, None] * col_scale[None, :]).astype(jnp.bfloat16)


def root_blocks(key, count):
    keys = jax.random.split(key, 4)
    noise = jnp.clip(jax.random.normal(keys[0], (count, BLK, BLK), jnp.float32), -4.0, 4.0)
    reach = 1.4
    strength = 1.0
    diag_scale = jnp.exp(jax.random.uniform(keys[1], (count, BLK), jnp.float32, -jnp.log(reach), jnp.log(reach)))
    left_factor = jax.random.uniform(keys[2], (count, BLK), jnp.float32, 0.5, 1.5)
    right_factor = jax.random.uniform(keys[3], (count, BLK), jnp.float32, 0.5, 1.5)
    eye_mask = (jnp.arange(BLK)[:, None] == jnp.arange(BLK)[None, :]).astype(jnp.float32)
    common = strength / BLK ** 0.5 * left_factor[:, :, None] * right_factor[:, None, :]
    return (diag_scale[:, :, None] * eye_mask[None] + noise * (0.35 / BLK ** 0.5) + common).astype(jnp.bfloat16)


def draw_left_roots(key, part):
    key = jax.random.fold_in(key, 23)
    return root_blocks(key, RBLK)


def draw_right_roots(key, part):
    key = jax.random.fold_in(key, 37)
    return root_blocks(key, CBLK)


def block_scale(rng, shape, shards, least, top_value):
    factor_of = 1.0
    for position, parts in shards:
        heights = jax.random.uniform(jax.random.fold_in(jax.random.fold_in(rng, 6), position), (parts,), jnp.float32, least / len(shards), top_value / len(shards))
        factor_of = factor_of * jnp.repeat(jnp.exp(heights), shape[position] // parts).reshape((-1,) + (1,) * (len(shape) - 1 - position))
    return factor_of


def setup_inputs(seed: int = 0) -> dict:
    seeds = jax.random.split(jax.random.key(seed), 5)
    return {
        "grad": draw_grad(jax.random.fold_in(seeds[4], 71), 0),
        "second_moment": jnp.clip(jnp.exp(math.log(5.0) - 4.6051702 * jax.random.uniform(seeds[1], (DW, FFW), jnp.float32) ** block_scale(seeds[1], (DW, FFW), ((0, 128), (1, 6)), -0.2, 0.2)), 0.05, 5.0),
        "left_roots": draw_left_roots(jax.random.fold_in(seeds[4], 71), 0),
        "right_roots": draw_right_roots(jax.random.fold_in(seeds[4], 71), 0),
    }


def block_squares(field):
    shaped = field.reshape(RBLK, BLK, CBLK, BLK)
    return lax.optimization_barrier(jnp.sum(shaped * shaped, axis=(1, 3)))

def reference(grad, second_moment, left_roots, right_roots):
    wide = grad.astype(jnp.float32)
    moment_next = 0.95 * second_moment + 0.05 * wide * wide
    adam = wide / (jnp.sqrt(moment_next) + 1e-08)
    split_cols = grad.reshape(DW, CBLK, BLK).astype(jnp.float32)
    projected = jnp.einsum('icj,cjk->ick', split_cols, right_roots.astype(jnp.float32))
    projected = projected.astype(jnp.bfloat16).reshape(RBLK, BLK, FFW)
    mixed = jnp.einsum('rij,rjk->rik', left_roots.astype(jnp.float32), projected.astype(jnp.float32))
    mixed = mixed.astype(jnp.bfloat16).reshape(DW, FFW).astype(jnp.float32)
    adam_sq = block_squares(adam)
    mixed_sq = block_squares(mixed)
    factor = jnp.sqrt(adam_sq) / (jnp.sqrt(mixed_sq) + 1e-06)
    scaled = mixed.reshape(RBLK, BLK, CBLK, BLK) * factor[:, None, :, None]
    update = scaled.reshape(DW, FFW).astype(jnp.bfloat16)
    return (update, moment_next)
```

```python
import jax
import jax.numpy as jnp
from jax import lax
from jax.sharding import Mesh, PartitionSpec as P

ZH, YY, XX = 4, 8, 4
PLANE = ("y", "x")
COLUMN = ("zh", "y")


def split3(value):
    high = lax.reduce_precision(value, 8, 7)
    rest = value - high
    middle = lax.reduce_precision(rest, 8, 7)
    return jnp.stack([high, middle, rest - middle], axis=-1)


def on_device(grad, second_moment, left_roots, right_roots):
    rows, width = grad.shape
    col_blocks, blk = right_roots.shape[:2]
    peers = YY * XX
    cols = width // YY
    sub = rows // XX
    send = jnp.broadcast_to(left_roots[:, None], (ZH, YY) + left_roots.shape[1:])
    send = send.reshape((ZH * YY,) + left_roots.shape[1:])
    left = lax.all_to_all(send, COLUMN, 0, 0, tiled=True).reshape(-1, blk)

    wide = grad.astype(jnp.float32)
    moment_next = 0.95 * second_moment + 0.05 * wide * wide
    adam = wide / (jnp.sqrt(moment_next) + 1e-08)
    adam_part = jnp.sum((adam * adam).reshape(rows, col_blocks, blk), axis=(0, 2))

    projected = jnp.concatenate(
        [
            jnp.dot(
                grad[:, c * blk : (c + 1) * blk],
                right_roots[c],
                preferred_element_type=jnp.float32,
            ).astype(jnp.bfloat16)
            for c in range(col_blocks)
        ],
        axis=1,
    )
    pieces = projected.reshape(rows, YY, cols).transpose(1, 0, 2)
    pieces = jnp.broadcast_to(pieces[:, None], (YY, XX, rows, cols))
    pieces = pieces.reshape(peers, rows, cols)
    tall = lax.all_to_all(pieces, PLANE, 0, 0, tiled=True).reshape(peers * rows, cols)

    mixed = jnp.dot(left, tall, preferred_element_type=jnp.float32).astype(jnp.bfloat16)
    again = mixed.astype(jnp.float32)
    mixed_part = jnp.sum(again * again)
    sums = split3(jnp.concatenate([mixed_part[None], adam_part])).reshape(-1)
    extra = jnp.zeros((8, 128), jnp.float32).at[0, : sums.shape[0]].set(sums)
    extra = jnp.broadcast_to(extra.astype(jnp.bfloat16), (peers, 8, 128))
    out = mixed.reshape(peers, sub, cols // 128, 128).transpose(0, 2, 1, 3)
    out = out.reshape(peers, -1, 128)
    n_out = out.shape[1]
    back = lax.all_to_all(jnp.concatenate([out, extra], axis=1), PLANE, 0, 0, tiled=True)

    sums = back[:, n_out, : 3 * (1 + col_blocks)].astype(jnp.float32)
    sums = sums.reshape(col_blocks, peers // col_blocks, 1 + col_blocks, 3).sum(axis=3)
    mixed_sq = jnp.sum(sums[:, :, 0], axis=1)
    adam_sq = jnp.sum(sums[:, :, 1:], axis=(0, 1))
    factor = jnp.sqrt(adam_sq) / (jnp.sqrt(mixed_sq) + 1e-06)
    result = back[:, :n_out].reshape(YY, XX, cols // 128, sub, 128)
    result = result.transpose(1, 3, 0, 2, 4).astype(jnp.float32)
    scaled = result * jnp.repeat(factor, YY // col_blocks)[None, None, :, None, None]
    update = scaled.astype(jnp.bfloat16).reshape(rows, width)
    return (update, moment_next)


def solution(mesh):
    tensor = mesh.shape["tensor"]
    fine = Mesh(mesh.devices.reshape(ZH, YY, XX, tensor), ("zh", "y", "x", "tensor"))
    dp = ("zh", "y", "x")
    return jax.shard_map(
        on_device,
        mesh=fine,
        in_specs=(
            P(dp, "tensor"),
            P(dp, "tensor"),
            P(None, dp, None),
            P("tensor", None, None),
        ),
        out_specs=(P(dp, "tensor"), P(dp, "tensor")),
        check_vma=False,
    )
```

```python
import jax
import jax.numpy as jnp
from jax import lax
from jax.sharding import Mesh, PartitionSpec as P

ZH, YY, XX = 4, 8, 4
PLANE = ("y", "x")


def split3(value):
    high = lax.reduce_precision(value, 8, 7)
    rest = value - high
    middle = lax.reduce_precision(rest, 8, 7)
    return jnp.stack([high, middle, rest - middle], axis=-1)


def on_device(grad, second_moment, left_roots, right_roots):
    rows, width = grad.shape
    col_blocks, blk = right_roots.shape[:2]
    peers = YY * XX
    cols = width // YY
    sub = rows // XX
    core = lax.axis_index("core")
    half = blk // 2
    mine = lax.dynamic_slice_in_dim(left_roots, core * half, half, axis=2)
    mine = lax.all_to_all(mine, "zh", 0, 0, tiled=True)
    n_left = ZH * mine.shape[1] * half // cols

    wide = grad.astype(jnp.float32)
    moment_next = 0.95 * second_moment + 0.05 * wide * wide
    adam = wide / (jnp.sqrt(moment_next) + 1e-08)
    adam_part = jnp.sum((adam * adam).reshape(rows, col_blocks, blk), axis=(0, 2))

    projected = jnp.concatenate(
        [
            jnp.dot(
                grad[:, c * blk : (c + 1) * blk],
                right_roots[c],
                preferred_element_type=jnp.float32,
            ).astype(jnp.bfloat16)
            for c in range(col_blocks)
        ],
        axis=1,
    )
    pieces = projected.reshape(rows, YY, cols).transpose(1, 0, 2)
    packed = mine.reshape(ZH, -1, half // cols, cols).transpose(0, 2, 1, 3)
    packed = jnp.broadcast_to(packed.reshape(1, n_left, cols), (YY, n_left, cols))
    got = lax.all_to_all(jnp.concatenate([pieces, packed], axis=1), "y", 0, 0, tiled=True)
    own = got[:, rows:]
    other = lax.ppermute(own, "core", [(0, 1), (1, 0)])
    strip = jnp.broadcast_to(got[None, :, :rows], (XX, YY, rows, cols))
    strip = lax.all_to_all(strip, "x", 0, 0, tiled=True)
    tall = strip.transpose(1, 0, 2, 3).reshape(peers * rows, cols)
    first = jnp.where(core == 0, own, other)
    second = jnp.where(core == 0, other, own)
    left = jnp.stack([first, second], axis=0).reshape(2, YY, ZH, half // cols, -1, cols)
    left = left.transpose(2, 1, 4, 0, 3, 5).reshape(-1, blk)

    mixed = jnp.dot(left, tall, preferred_element_type=jnp.float32).astype(jnp.bfloat16)
    again = mixed.astype(jnp.float32)
    mixed_part = jnp.sum(again * again)
    sums = split3(jnp.concatenate([mixed_part[None], adam_part])).reshape(-1)
    extra = jnp.zeros((8, 128), jnp.float32).at[0, : sums.shape[0]].set(sums)
    extra = jnp.broadcast_to(extra.astype(jnp.bfloat16), (peers, 8, 128))
    out = mixed.reshape(peers, sub, cols // 128, 128).transpose(0, 2, 1, 3)
    out = out.reshape(peers, -1, 128)
    n_out = out.shape[1]
    back = lax.all_to_all(jnp.concatenate([out, extra], axis=1), PLANE, 0, 0, tiled=True)

    sums = back[:, n_out, : 3 * (1 + col_blocks)].astype(jnp.float32)
    sums = sums.reshape(col_blocks, peers // col_blocks, 1 + col_blocks, 3).sum(axis=3)
    mixed_sq = jnp.sum(sums[:, :, 0], axis=1)
    adam_sq = jnp.sum(sums[:, :, 1:], axis=(0, 1))
    factor = jnp.sqrt(adam_sq) / (jnp.sqrt(mixed_sq) + 1e-06)
    result = back[:, :n_out].reshape(YY, XX, cols // 128, sub, 128)
    result = result.transpose(1, 3, 0, 2, 4).astype(jnp.float32)
    scaled = result * jnp.repeat(factor, YY // col_blocks)[None, None, :, None, None]
    update = scaled.astype(jnp.bfloat16).reshape(rows, width)
    return (update, moment_next)


def solution(mesh):
    tensor = mesh.shape["tensor"]
    cores = 2 if tensor % 2 == 0 else 1
    names = ("zh", "y", "x", "zl", "core")
    fine = Mesh(mesh.devices.reshape(ZH, YY, XX, tensor // cores, cores), names)
    dp, columns = ("zh", "y", "x"), ("zl", "core")
    return jax.shard_map(
        on_device,
        mesh=fine,
        in_specs=(
            P(dp, columns),
            P(dp, columns),
            P(None, dp, None),
            P(columns, None, None),
        ),
        out_specs=(P(dp, columns), P(dp, columns)),
        check_vma=False,
    )
```

```python
import jax
import jax.numpy as jnp
from jax import lax
from jax.experimental import pallas as pl
from jax.experimental.pallas import tpu as pltpu
from jax.sharding import Mesh, PartitionSpec as P

ZH, YY, XX = 4, 8, 4
PEERS = YY * XX
PLANE = ("y", "x")
LANES = 128
F32, BF16 = jnp.float32, jnp.bfloat16
WHOLE = pl.BlockSpec(memory_space=pltpu.VMEM)


def split3(value):
    high = value.astype(BF16).astype(F32)
    rest = value - high
    middle = rest.astype(BF16).astype(F32)
    return high, middle, rest - middle


def by_lane(values, shape):
    lane = lax.broadcasted_iota(jnp.int32, shape, len(shape) - 1)
    out = jnp.zeros(shape, F32)
    for i, value in enumerate(values):
        out = jnp.where(lane == i, value, out)
    return out


def swap_rows(groups):
    n = 32 * groups
    row = lax.broadcasted_iota(jnp.int32, (n, n), 0)
    col = lax.broadcasted_iota(jnp.int32, (n, n), 1)
    if groups == 1:
        want = ((row >> 1) & 3) * 8 + (row >> 3) * 2 + (row & 1)
    else:
        want = ((row >> 3) & 7) * 32 + ((row >> 1) & 3) * 8 + (row >> 6) * 2 + (row & 1)
    return (col == want).astype(BF16)


def pack_kernel(proj_ref, left_ref, perm_ref, out_ref):
    rows, width = proj_ref.shape
    cols = width // YY
    blk = left_ref.shape[2]
    flat = left_ref[...].reshape(rows, blk)
    left = jnp.dot(perm_ref[...], flat, preferred_element_type=F32)
    sub = rows // XX
    for q in range(XX):
        piece = left[q * sub : (q + 1) * sub]
        tall = [piece[:, h * cols : (h + 1) * cols] for h in range(blk // cols)]
        piece = jnp.concatenate(tall, axis=0).astype(BF16)
        for j in range(YY):
            out_ref[j * XX + q, rows:, :] = piece
    for j in range(YY):
        piece = proj_ref[:, j * cols : (j + 1) * cols]
        for q in range(XX):
            out_ref[j * XX + q, :rows, :] = piece


def product_kernel(got_ref, perm_ref, adam_ref, out_ref):
    peers, both, cols = got_ref.shape
    rows = both // 2
    sub = rows // XX
    tall = got_ref[:, :rows, :].reshape(peers * rows, cols)
    total = jnp.zeros((peers * sub, cols), F32)
    for g in range(2):
        pair = got_ref[:, rows + g * 16 : rows + (g + 1) * 16, :].reshape(peers * 16, cols)
        for h in range(2):
            k = (2 * g + h) * cols
            part = jnp.dot(pair, tall[k : k + cols], preferred_element_type=F32)
            part = part.reshape(peers, 2, sub, cols)[:, h]
            total = total + part.reshape(peers * sub, cols)
    mixed = total.astype(BF16)
    again = mixed.astype(F32)
    square = jnp.sum(jnp.sum(again * again, axis=0, keepdims=True), axis=1, keepdims=True)
    sums = by_lane(split3(square), (1, LANES)) + adam_ref[...]
    out_ref[:, :, cols:] = jnp.broadcast_to(sums.astype(BF16)[None], (peers, sub, LANES))
    turned = jnp.dot(perm_ref[...], mixed, preferred_element_type=F32).astype(BF16)
    out_ref[:, :, :cols] = turned.reshape(peers, sub, cols)


def update_kernel(col_blocks, back_ref, perm_ref, out_ref):
    peers, sub, both = back_ref.shape
    cols = both - LANES
    back = back_ref[...].astype(F32)
    sums = back[:, 0, cols:]
    lane = lax.broadcasted_iota(jnp.int32, (1, LANES), 1)
    every = jnp.sum(sums, axis=0, keepdims=True)
    share = peers // col_blocks
    for c in range(col_blocks):
        own = jnp.sum(sums[c * share : (c + 1) * share], axis=0, keepdims=True)
        mixed_sq = jnp.sum(jnp.where(lane < 3, own, 0.0), axis=1, keepdims=True)
        here = (lane >= 3 * (c + 1)) & (lane < 3 * (c + 2))
        adam_sq = jnp.sum(jnp.where(here, every, 0.0), axis=1, keepdims=True)
        factor = jnp.sqrt(adam_sq) / (jnp.sqrt(mixed_sq) + 1e-06)
        for j in range(c * YY // col_blocks, (c + 1) * YY // col_blocks):
            piece = back[j * XX : (j + 1) * XX, :, :cols].reshape(XX * sub, cols)
            piece = jnp.dot(perm_ref[...], piece.astype(BF16), preferred_element_type=F32)
            out_ref[:, j * cols : (j + 1) * cols] = (piece * factor).astype(BF16)


def on_device(grad, second_moment, left_roots, right_roots):
    rows, width = grad.shape
    col_blocks, blk = right_roots.shape[:2]
    cols = width // YY
    sub = rows // XX
    mine = lax.all_to_all(left_roots, "zh", 0, 0, tiled=True)

    projected = jnp.concatenate(
        [
            jnp.dot(
                grad[:, c * blk : (c + 1) * blk],
                right_roots[c],
                preferred_element_type=F32,
            ).astype(BF16)
            for c in range(col_blocks)
        ],
        axis=1,
    )
    wide = grad.astype(F32)
    moment_next = 0.95 * second_moment + 0.05 * wide * wide
    adam = wide / (jnp.sqrt(moment_next) + 1e-08)
    adam_part = jnp.sum((adam * adam).reshape(rows, col_blocks, blk), axis=(0, 2))
    high = lax.reduce_precision(adam_part, 8, 7)
    middle = lax.reduce_precision(adam_part - high, 8, 7)
    adam_sums = jnp.stack([high, middle, adam_part - high - middle], axis=1).reshape(1, -1)
    adam_sums = jnp.pad(adam_sums, ((0, 0), (3, LANES - 3 - adam_sums.shape[1])))

    send = pl.pallas_call(
        pack_kernel,
        out_shape=jax.ShapeDtypeStruct((PEERS, 2 * rows, cols), BF16),
        in_specs=[WHOLE] * 3,
        out_specs=WHOLE,
        name="pack",
        cost_estimate=pl.CostEstimate(flops=2**21, bytes_accessed=2**21, transcendentals=0),
    )(projected, mine, swap_rows(1))
    got = lax.all_to_all(send, PLANE, 0, 0, tiled=True)
    ready = pl.pallas_call(
        product_kernel,
        out_shape=jax.ShapeDtypeStruct((PEERS, sub, cols + LANES), BF16),
        in_specs=[WHOLE] * 3,
        out_specs=WHOLE,
        name="product",
        cost_estimate=pl.CostEstimate(flops=2**28, bytes_accessed=2**21, transcendentals=0),
    )(got, swap_rows(YY), adam_sums)
    back = lax.all_to_all(ready, PLANE, 0, 0, tiled=True)
    update = pl.pallas_call(
        lambda *refs: update_kernel(col_blocks, *refs),
        out_shape=jax.ShapeDtypeStruct((rows, width), BF16),
        in_specs=[WHOLE] * 2,
        out_specs=WHOLE,
        name="update",
        cost_estimate=pl.CostEstimate(flops=2**22, bytes_accessed=2**19, transcendentals=0),
    )(back, swap_rows(1))
    return (update, moment_next)


def solution(mesh):
    tensor = mesh.shape["tensor"]
    fine = Mesh(mesh.devices.reshape(ZH, YY, XX, tensor), ("zh", "y", "x", "tensor"))
    dp = ("zh", "y", "x")
    return jax.shard_map(
        on_device,
        mesh=fine,
        in_specs=(
            P(dp, "tensor"),
            P(dp, "tensor"),
            P(None, dp, None),
            P("tensor", None, None),
        ),
        out_specs=(P(dp, "tensor"), P(dp, "tensor")),
        check_vma=False,
    )
```

```python
import jax
import jax.numpy as jnp
from jax import lax
from jax.experimental import pallas as pl
from jax.experimental.pallas import tpu as pltpu
from jax.sharding import Mesh, PartitionSpec as P

ZH, YY, XX = 4, 8, 4
PEERS = YY * XX
PLANE = ("y", "x")
LANES = 128
F32, BF16 = jnp.float32, jnp.bfloat16
SMALL = pltpu.CompilerParams(vmem_limit_bytes=16 * 2**20)
WHOLE = pl.BlockSpec(memory_space=pltpu.VMEM)


def split3(value):
    high = value.astype(BF16).astype(F32)
    rest = value - high
    middle = rest.astype(BF16).astype(F32)
    return high, middle, rest - middle


def by_lane(values, shape):
    lane = lax.broadcasted_iota(jnp.int32, shape, len(shape) - 1)
    out = jnp.zeros(shape, F32)
    for i, value in enumerate(values):
        out = jnp.where(lane == i, value, out)
    return out


def right_kernel(grad_ref, right_ref, out_ref):
    both = jnp.dot(grad_ref[...], right_ref[0], preferred_element_type=F32).astype(BF16)
    cols = out_ref.shape[2]
    for i in range(both.shape[1] // cols):
        out_ref[i] = both[:, i * cols : (i + 1) * cols]


def pack_kernel(piece_ref, left_ref, out_ref):
    rows, cols = piece_ref.shape[1:]
    planes, sub, blk = left_ref.shape
    n = planes * sub
    left = left_ref[...].reshape(n, blk)
    for j in range(YY):
        out_ref[j, :rows] = piece_ref[j]
        for h in range(blk // cols):
            out_ref[j, rows + h * n : rows + (h + 1) * n] = left[:, h * cols : (h + 1) * cols]


def product_kernel(strip_ref, got_ref, adam_ref, out_ref):
    rows, cols = strip_ref.shape[2:]
    sub = rows // XX
    n = ZH * sub
    steps = (got_ref.shape[1] - rows) // n
    total = jnp.zeros((YY * n, cols), F32)
    for h in range(steps):
        left = got_ref[:, rows + h * n : rows + (h + 1) * n, :].reshape(YY * n, cols)
        per = cols // (XX * rows)
        tall = [strip_ref[i, h * per + j] for j in range(per) for i in range(XX)]
        tall = jnp.concatenate(tall, axis=0)
        total = total + jnp.dot(left, tall, preferred_element_type=F32)
    mixed = total.astype(BF16).astype(F32)
    square = jnp.sum(jnp.sum(mixed * mixed, axis=0, keepdims=True), axis=1, keepdims=True)
    sums = by_lane(split3(square), (1, LANES)) + adam_ref[...]
    sums = jnp.broadcast_to(sums, (sub, LANES))
    for y in range(YY):
        for z in range(ZH):
            m = (y * ZH + z) * sub
            piece = jnp.concatenate([mixed[m : m + sub], sums], axis=1)
            out_ref[z * YY + y] = piece.astype(BF16)


def update_kernel(col_blocks, back_ref, out_ref):
    peers, sub, both = back_ref.shape
    cols = both - LANES
    back = back_ref[...].astype(F32)
    sums = back[:, 0, cols:]
    lane = lax.broadcasted_iota(jnp.int32, (1, LANES), 1)
    every = jnp.sum(sums, axis=0, keepdims=True)
    share = peers // col_blocks
    for c in range(col_blocks):
        own = jnp.sum(sums[c * share : (c + 1) * share], axis=0, keepdims=True)
        mixed_sq = jnp.sum(jnp.where(lane < 3, own, 0.0), axis=1, keepdims=True)
        here = (lane >= 3 * (c + 1)) & (lane < 3 * (c + 2))
        adam_sq = jnp.sum(jnp.where(here, every, 0.0), axis=1, keepdims=True)
        factor = jnp.sqrt(adam_sq) / (jnp.sqrt(mixed_sq) + 1e-06)
        for j in range(c * YY // col_blocks, (c + 1) * YY // col_blocks):
            piece = back[j * XX : (j + 1) * XX, :, :cols].reshape(XX * sub, cols)
            out_ref[:, j * cols : (j + 1) * cols] = (piece * factor).astype(BF16)


def on_device(grad, second_moment, left_roots, right_roots):
    rows, width = grad.shape
    col_blocks, blk = right_roots.shape[:2]
    cols = width // YY
    sub = rows // XX
    mine = lax.all_to_all(left_roots, "zh", 0, 0, tiled=True)
    wide_cols = width // 4
    per_block = blk // wide_cols
    pieces = pl.pallas_call(
        right_kernel,
        grid=(4,),
        out_shape=jax.ShapeDtypeStruct((YY, rows, cols), BF16),
        in_specs=[
            pl.BlockSpec((rows, blk), lambda s: (0, s // per_block)),
            pl.BlockSpec((1, blk, wide_cols), lambda s: (s // per_block, 0, s % per_block)),
        ],
        out_specs=pl.BlockSpec((YY // 4, rows, cols), lambda s: (s, 0, 0)),
        name="right",
        compiler_params=pltpu.CompilerParams(vmem_limit_bytes=57 * 2**20),
        cost_estimate=pl.CostEstimate(flops=2**27, bytes_accessed=2**22, transcendentals=0),
    )(grad, right_roots)
    wide = grad.astype(F32)
    moment_next = 0.95 * second_moment + 0.05 * wide * wide
    adam = wide / (jnp.sqrt(moment_next) + 1e-08)
    adam_part = jnp.sum((adam * adam).reshape(rows, col_blocks, blk), axis=(0, 2))
    high = lax.reduce_precision(adam_part, 8, 7)
    middle = lax.reduce_precision(adam_part - high, 8, 7)
    adam_sums = jnp.stack([high, middle, adam_part - high - middle], axis=1).reshape(1, -1)
    adam_sums = jnp.pad(adam_sums, ((0, 0), (3, LANES - 3 - adam_sums.shape[1])))

    send = pl.pallas_call(
        pack_kernel,
        out_shape=jax.ShapeDtypeStruct((YY, rows + ZH * sub * blk // cols, cols), BF16),
        in_specs=[WHOLE] * 2,
        out_specs=WHOLE,
        name="pack",
        compiler_params=SMALL,
        cost_estimate=pl.CostEstimate(flops=2**10, bytes_accessed=2**20, transcendentals=0),
    )(pieces, mine)
    got = lax.all_to_all(send, "y", 0, 0, tiled=True)
    strip = jnp.broadcast_to(got[None, :, :rows], (XX, YY, rows, cols))
    strip = lax.all_to_all(strip, "x", 0, 0, tiled=True)
    ready = pl.pallas_call(
        product_kernel,
        out_shape=jax.ShapeDtypeStruct((PEERS, sub, cols + LANES), BF16),
        in_specs=[WHOLE] * 3,
        out_specs=WHOLE,
        name="product",
        compiler_params=SMALL,
        cost_estimate=pl.CostEstimate(flops=2**28, bytes_accessed=2**21, transcendentals=0),
    )(strip, got, adam_sums)
    back = lax.all_to_all(ready, PLANE, 0, 0, tiled=True)
    update = pl.pallas_call(
        lambda *refs: update_kernel(col_blocks, *refs),
        out_shape=jax.ShapeDtypeStruct((rows, width), BF16),
        in_specs=[WHOLE],
        out_specs=WHOLE,
        name="update",
        compiler_params=SMALL,
        cost_estimate=pl.CostEstimate(flops=2**22, bytes_accessed=2**19, transcendentals=0),
    )(back)
    return (update, moment_next)


def solution(mesh):
    tensor = mesh.shape["tensor"]
    fine = Mesh(mesh.devices.reshape(ZH, YY, XX, tensor), ("zh", "y", "x", "tensor"))
    dp = ("zh", "y", "x")
    return jax.shard_map(
        on_device,
        mesh=fine,
        in_specs=(
            P(dp, "tensor"),
            P(dp, "tensor"),
            P(None, dp, None),
            P("tensor", None, None),
        ),
        out_specs=(P(dp, "tensor"), P(dp, "tensor")),
        check_vma=False,
    )
```

```python
import jax
import jax.numpy as jnp
from jax import lax
from jax.experimental import pallas as pl
from jax.experimental.pallas import tpu as pltpu
from jax.sharding import Mesh, PartitionSpec as P

ZH, YY, XX = 4, 8, 4
PEERS = YY * XX
PLANE = ("y", "x")
LANES = 128
F32, BF16 = jnp.float32, jnp.bfloat16
SMALL = pltpu.CompilerParams(vmem_limit_bytes=16 * 2**20)
SCALARS = pl.BlockSpec(memory_space=pltpu.SMEM)
WHOLE = pl.BlockSpec(memory_space=pltpu.VMEM)


def split3(value):
    high = value.astype(BF16).astype(F32)
    rest = value - high
    middle = rest.astype(BF16).astype(F32)
    return high, middle, rest - middle


def by_lane(values, shape):
    lane = lax.broadcasted_iota(jnp.int32, shape, len(shape) - 1)
    out = jnp.zeros(shape, F32)
    for i, value in enumerate(values):
        out = jnp.where(lane == i, value, out)
    return out


def right_kernel(grad_ref, right_ref, out_ref):
    both = jnp.dot(grad_ref[...], right_ref[0], preferred_element_type=F32).astype(BF16)
    cols = out_ref.shape[2]
    for i in range(both.shape[1] // cols):
        out_ref[i] = both[:, i * cols : (i + 1) * cols]


def pack_kernel(core_ref, piece_ref, left_ref, out_ref):
    rows, cols = piece_ref.shape[1:]
    planes, sub, blk = left_ref.shape
    n = planes * sub
    half = blk // 2
    left = left_ref[...].reshape(n, blk)
    left = jnp.where(core_ref[0] == 0, left[:, :half], left[:, half:])
    for j in range(YY):
        out_ref[j, :rows] = piece_ref[j]
        for h in range(half // cols):
            out_ref[j, rows + h * n : rows + (h + 1) * n] = left[:, h * cols : (h + 1) * cols]


def product_kernel(strip_ref, left_ref, adam_ref, out_ref):
    rows, cols = strip_ref.shape[2:]
    sub = rows // XX
    n = ZH * sub
    steps = left_ref.shape[2] // n
    per = cols // (XX * rows)
    total = jnp.zeros((YY * n, cols), F32)
    for h in range(2 * steps):
        left = left_ref[h // steps, :, h % steps * n : (h % steps + 1) * n, :]
        tall = [strip_ref[i, h * per + j] for j in range(per) for i in range(XX)]
        tall = jnp.concatenate(tall, axis=0)
        total = total + jnp.dot(left.reshape(YY * n, cols), tall, preferred_element_type=F32)
    mixed = total.astype(BF16).astype(F32)
    square = jnp.sum(jnp.sum(mixed * mixed, axis=0, keepdims=True), axis=1, keepdims=True)
    sums = by_lane(split3(square), (1, LANES)) + adam_ref[...]
    sums = jnp.broadcast_to(sums, (sub, LANES))
    for y in range(YY):
        for z in range(ZH):
            m = (y * ZH + z) * sub
            piece = jnp.concatenate([mixed[m : m + sub], sums], axis=1)
            out_ref[z * YY + y] = piece.astype(BF16)


def update_kernel(col_blocks, back_ref, out_ref):
    peers, sub, both = back_ref.shape
    cols = both - LANES
    back = back_ref[...].astype(F32)
    sums = back[:, 0, cols:]
    lane = lax.broadcasted_iota(jnp.int32, (1, LANES), 1)
    every = jnp.sum(sums, axis=0, keepdims=True)
    share = peers // col_blocks
    for c in range(col_blocks):
        own = jnp.sum(sums[c * share : (c + 1) * share], axis=0, keepdims=True)
        mixed_sq = jnp.sum(jnp.where(lane < 3, own, 0.0), axis=1, keepdims=True)
        here = (lane >= 3 * (c + 1)) & (lane < 3 * (c + 2))
        adam_sq = jnp.sum(jnp.where(here, every, 0.0), axis=1, keepdims=True)
        factor = jnp.sqrt(adam_sq) / (jnp.sqrt(mixed_sq) + 1e-06)
        for j in range(c * YY // col_blocks, (c + 1) * YY // col_blocks):
            piece = back[j * XX : (j + 1) * XX, :, :cols].reshape(XX * sub, cols)
            out_ref[:, j * cols : (j + 1) * cols] = (piece * factor).astype(BF16)


def on_device(grad, second_moment, left_roots, right_roots):
    rows, width = grad.shape
    col_blocks, blk = right_roots.shape[:2]
    cols = width // YY
    sub = rows // XX
    mine = lax.all_to_all(left_roots, "zh", 0, 0, tiled=True)
    wide_cols = width // 4
    per_block = blk // wide_cols
    pieces = pl.pallas_call(
        right_kernel,
        grid=(4,),
        out_shape=jax.ShapeDtypeStruct((YY, rows, cols), BF16),
        in_specs=[
            pl.BlockSpec((rows, blk), lambda s: (0, s // per_block)),
            pl.BlockSpec((1, blk, wide_cols), lambda s: (s // per_block, 0, s % per_block)),
        ],
        out_specs=pl.BlockSpec((YY // 4, rows, cols), lambda s: (s, 0, 0)),
        name="right",
        compiler_params=SMALL,
        cost_estimate=pl.CostEstimate(flops=2**27, bytes_accessed=2**22, transcendentals=0),
    )(grad, right_roots)
    wide = grad.astype(F32)
    moment_next = 0.95 * second_moment + 0.05 * wide * wide
    adam = wide / (jnp.sqrt(moment_next) + 1e-08)
    adam_part = jnp.sum((adam * adam).reshape(rows, col_blocks, blk), axis=(0, 2))
    high = lax.reduce_precision(adam_part, 8, 7)
    middle = lax.reduce_precision(adam_part - high, 8, 7)
    adam_sums = jnp.stack([high, middle, adam_part - high - middle], axis=1).reshape(1, -1)
    adam_sums = jnp.pad(adam_sums, ((0, 0), (3, LANES - 3 - adam_sums.shape[1])))

    send = pl.pallas_call(
        pack_kernel,
        out_shape=jax.ShapeDtypeStruct((YY, rows + ZH * sub * blk // (2 * cols), cols), BF16),
        in_specs=[SCALARS] + [WHOLE] * 2,
        out_specs=WHOLE,
        name="pack",
        compiler_params=SMALL,
        cost_estimate=pl.CostEstimate(flops=2**10, bytes_accessed=2**20, transcendentals=0),
    )(lax.axis_index("core")[None], pieces, mine)
    got = lax.all_to_all(send, "y", 0, 0, tiled=True)
    left = lax.all_gather(got[:, rows:], "core", axis=0)
    strip = jnp.broadcast_to(got[None, :, :rows], (XX, YY, rows, cols))
    strip = lax.all_to_all(strip, "x", 0, 0, tiled=True)
    ready = pl.pallas_call(
        product_kernel,
        out_shape=jax.ShapeDtypeStruct((PEERS, sub, cols + LANES), BF16),
        in_specs=[WHOLE] * 3,
        out_specs=WHOLE,
        name="product",
        compiler_params=SMALL,
        cost_estimate=pl.CostEstimate(flops=2**28, bytes_accessed=2**21, transcendentals=0),
    )(strip, left, adam_sums)
    back = lax.all_to_all(ready, PLANE, 0, 0, tiled=True)
    update = pl.pallas_call(
        lambda *refs: update_kernel(col_blocks, *refs),
        out_shape=jax.ShapeDtypeStruct((rows, width), BF16),
        in_specs=[WHOLE],
        out_specs=WHOLE,
        name="update",
        compiler_params=SMALL,
        cost_estimate=pl.CostEstimate(flops=2**22, bytes_accessed=2**19, transcendentals=0),
    )(back)
    return (update, moment_next)


def solution(mesh):
    tensor = mesh.shape["tensor"]
    names = ("zh", "y", "x", "zl", "core")
    fine = Mesh(mesh.devices.reshape(ZH, YY, XX, tensor // 2, 2), names)
    dp, columns = ("zh", "y", "x"), ("zl", "core")
    return jax.shard_map(
        on_device,
        mesh=fine,
        in_specs=(
            P(dp, columns),
            P(dp, columns),
            P(None, dp, None),
            P(columns, None, None),
        ),
        out_specs=(P(dp, columns), P(dp, columns)),
        check_vma=False,
    )
```

```python
import functools

import jax
import jax.numpy as jnp
from jax import lax
from jax.experimental import pallas as pl
from jax.experimental.pallas import tpu as pltpu
from jax.sharding import Mesh, PartitionSpec as P

ZH, YY, XX = 4, 8, 4
PEERS = YY * XX
PLANE = ("y", "x")
LANES = 128
F32, BF16 = jnp.float32, jnp.bfloat16
SMALL = pltpu.CompilerParams(vmem_limit_bytes=16 * 2**20)
SCALARS = pl.BlockSpec(memory_space=pltpu.SMEM)
WHOLE = pl.BlockSpec(memory_space=pltpu.VMEM)


def split3(value):
    high = value.astype(BF16).astype(F32)
    rest = value - high
    middle = rest.astype(BF16).astype(F32)
    return high, middle, rest - middle


def by_lane(values, shape):
    lane = lax.broadcasted_iota(jnp.int32, shape, len(shape) - 1)
    out = jnp.zeros(shape, F32)
    for i, value in enumerate(values):
        out = jnp.where(lane == i, value, out)
    return out


def right_kernel(
    col_blocks, grad_ref, right_ref, part_ref, moment_ref, out_ref, next_ref, sums_ref, held_ref
):
    step = pl.program_id(0)
    steps = pl.num_programs(0)
    both = jnp.dot(grad_ref[...], right_ref[0], preferred_element_type=F32).astype(BF16)
    cols = out_ref.shape[2]
    for i in range(both.shape[1] // cols):
        out_ref[i] = both[:, i * cols : (i + 1) * cols]
    wide = part_ref[...].astype(F32)
    moment_next = 0.95 * moment_ref[...] + 0.05 * wide * wide
    next_ref[...] = moment_next
    adam = wide / (jnp.sqrt(moment_next) + 1e-08)
    square = jnp.sum(jnp.sum(adam * adam, axis=0, keepdims=True), axis=1, keepdims=True)
    held_ref[step] = jnp.broadcast_to(square, held_ref.shape[1:])

    @pl.when(step == steps - 1)
    def _():
        count = held_ref.shape[0] // col_blocks
        values = []
        for c in range(col_blocks):
            total = held_ref[c * count]
            for i in range(1, count):
                total = total + held_ref[c * count + i]
            values += split3(total)
        lane = lax.broadcasted_iota(jnp.int32, sums_ref.shape, 1)
        out = jnp.zeros(sums_ref.shape, F32)
        for i, value in enumerate(values):
            out = jnp.where(lane == 3 + i, value, out)
        sums_ref[...] = out


def pack_kernel(core_ref, piece_ref, left_ref, out_ref):
    rows, cols = piece_ref.shape[1:]
    planes, sub, blk = left_ref.shape
    n = planes * sub
    half = blk // 2
    left = left_ref[...].reshape(n, blk)
    left = jnp.where(core_ref[0] == 0, left[:, :half], left[:, half:])
    for j in range(YY):
        out_ref[j, :rows] = piece_ref[j]
        for h in range(half // cols):
            out_ref[j, rows + h * n : rows + (h + 1) * n] = left[:, h * cols : (h + 1) * cols]


def product_kernel(strip_ref, left_ref, adam_ref, out_ref):
    rows, cols = strip_ref.shape[2:]
    sub = rows // XX
    n = ZH * sub
    steps = left_ref.shape[2] // n
    per = cols // (XX * rows)
    total = jnp.zeros((YY * n, cols), F32)
    for h in range(2 * steps):
        left = left_ref[h // steps, :, h % steps * n : (h % steps + 1) * n, :]
        tall = [strip_ref[i, h * per + j] for j in range(per) for i in range(XX)]
        tall = jnp.concatenate(tall, axis=0)
        total = total + jnp.dot(left.reshape(YY * n, cols), tall, preferred_element_type=F32)
    mixed = total.astype(BF16).astype(F32)
    square = jnp.sum(jnp.sum(mixed * mixed, axis=0, keepdims=True), axis=1, keepdims=True)
    sums = by_lane(split3(square), (1, LANES)) + adam_ref[...]
    sums = jnp.broadcast_to(sums, (sub, LANES))
    for y in range(YY):
        for z in range(ZH):
            m = (y * ZH + z) * sub
            piece = jnp.concatenate([mixed[m : m + sub], sums], axis=1)
            out_ref[z * YY + y] = piece.astype(BF16)


def update_kernel(col_blocks, back_ref, out_ref):
    peers, sub, both = back_ref.shape
    cols = both - LANES
    back = back_ref[...].astype(F32)
    sums = back[:, 0, cols:]
    lane = lax.broadcasted_iota(jnp.int32, (1, LANES), 1)
    every = jnp.sum(sums, axis=0, keepdims=True)
    share = peers // col_blocks
    for c in range(col_blocks):
        own = jnp.sum(sums[c * share : (c + 1) * share], axis=0, keepdims=True)
        mixed_sq = jnp.sum(jnp.where(lane < 3, own, 0.0), axis=1, keepdims=True)
        here = (lane >= 3 * (c + 1)) & (lane < 3 * (c + 2))
        adam_sq = jnp.sum(jnp.where(here, every, 0.0), axis=1, keepdims=True)
        factor = jnp.sqrt(adam_sq) / (jnp.sqrt(mixed_sq) + 1e-06)
        for j in range(c * YY // col_blocks, (c + 1) * YY // col_blocks):
            piece = back[j * XX : (j + 1) * XX, :, :cols].reshape(XX * sub, cols)
            out_ref[:, j * cols : (j + 1) * cols] = (piece * factor).astype(BF16)


def on_device(grad, second_moment, left_roots, right_roots):
    rows, width = grad.shape
    col_blocks, blk = right_roots.shape[:2]
    cols = width // YY
    sub = rows // XX
    mine = lax.all_to_all(left_roots, "zh", 0, 0, tiled=True)
    wide_cols = width // 4
    per_block = blk // wide_cols
    tile = lambda s: (0, s)
    pieces, moment_next, adam_sums = pl.pallas_call(
        functools.partial(right_kernel, col_blocks),
        grid=(4,),
        out_shape=(
            jax.ShapeDtypeStruct((YY, rows, cols), BF16),
            jax.ShapeDtypeStruct((rows, width), F32),
            jax.ShapeDtypeStruct((1, LANES), F32),
        ),
        in_specs=[
            pl.BlockSpec((rows, blk), lambda s: (0, s // per_block)),
            pl.BlockSpec((1, blk, wide_cols), lambda s: (s // per_block, 0, s % per_block)),
            pl.BlockSpec((rows, wide_cols), tile),
            pl.BlockSpec((rows, wide_cols), tile),
        ],
        out_specs=(
            pl.BlockSpec((YY // 4, rows, cols), lambda s: (s, 0, 0)),
            pl.BlockSpec((rows, wide_cols), tile),
            pl.BlockSpec((1, LANES), lambda s: (0, 0)),
        ),
        scratch_shapes=[pltpu.VMEM((4, 1, LANES), F32)],
        name="right",
        compiler_params=SMALL,
        cost_estimate=pl.CostEstimate(flops=2**27, bytes_accessed=2**22, transcendentals=2**16),
    )(grad, right_roots, grad, second_moment)
    send = pl.pallas_call(
        pack_kernel,
        out_shape=jax.ShapeDtypeStruct((YY, rows + ZH * sub * blk // (2 * cols), cols), BF16),
        in_specs=[SCALARS] + [WHOLE] * 2,
        out_specs=WHOLE,
        name="pack",
        compiler_params=SMALL,
        cost_estimate=pl.CostEstimate(flops=2**10, bytes_accessed=2**20, transcendentals=0),
    )(lax.axis_index("core")[None], pieces, mine)
    got = lax.all_to_all(send, "y", 0, 0, tiled=True)
    left = lax.all_gather(got[:, rows:], "core", axis=0)
    strip = jnp.broadcast_to(got[None, :, :rows], (XX, YY, rows, cols))
    strip = lax.all_to_all(strip, "x", 0, 0, tiled=True)
    ready = pl.pallas_call(
        product_kernel,
        out_shape=jax.ShapeDtypeStruct((PEERS, sub, cols + LANES), BF16),
        in_specs=[WHOLE] * 3,
        out_specs=WHOLE,
        name="product",
        compiler_params=SMALL,
        cost_estimate=pl.CostEstimate(flops=2**28, bytes_accessed=2**21, transcendentals=0),
    )(strip, left, adam_sums)
    back = lax.all_to_all(ready, PLANE, 0, 0, tiled=True)
    update = pl.pallas_call(
        functools.partial(update_kernel, col_blocks),
        out_shape=jax.ShapeDtypeStruct((rows, width), BF16),
        in_specs=[WHOLE],
        out_specs=WHOLE,
        name="update",
        compiler_params=SMALL,
        cost_estimate=pl.CostEstimate(flops=2**22, bytes_accessed=2**19, transcendentals=0),
    )(back)
    return (update, moment_next)


def solution(mesh):
    tensor = mesh.shape["tensor"]
    names = ("zh", "y", "x", "zl", "core")
    fine = Mesh(mesh.devices.reshape(ZH, YY, XX, tensor // 2, 2), names)
    dp, columns = ("zh", "y", "x"), ("zl", "core")
    return jax.shard_map(
        on_device,
        mesh=fine,
        in_specs=(
            P(dp, columns),
            P(dp, columns),
            P(None, dp, None),
            P(columns, None, None),
        ),
        out_specs=(P(dp, columns), P(dp, columns)),
        check_vma=False,
    )
```

```python
import functools

import jax
import jax.numpy as jnp
from jax import lax
from jax.experimental import pallas as pl
from jax.experimental.pallas import tpu as pltpu
from jax.sharding import Mesh, PartitionSpec as P

ZH, YY, XX = 4, 8, 4
PEERS = YY * XX
PLANE = ("y", "x")
LANES = 128
F32, BF16 = jnp.float32, jnp.bfloat16
SMALL = pltpu.CompilerParams(vmem_limit_bytes=16 * 2**20)
SCALARS = pl.BlockSpec(memory_space=pltpu.SMEM)
WHOLE = pl.BlockSpec(memory_space=pltpu.VMEM)


def split3(value):
    high = value.astype(BF16).astype(F32)
    rest = value - high
    middle = rest.astype(BF16).astype(F32)
    return high, middle, rest - middle


def by_lane(values, shape):
    lane = lax.broadcasted_iota(jnp.int32, shape, len(shape) - 1)
    out = jnp.zeros(shape, F32)
    for i, value in enumerate(values):
        out = jnp.where(lane == i, value, out)
    return out


def right_kernel(
    col_blocks, grad_ref, right_ref, part_ref, moment_ref, out_ref, next_ref, sums_ref, held_ref
):
    step = pl.program_id(0)
    steps = pl.num_programs(0)
    both = jnp.dot(grad_ref[...], right_ref[0], preferred_element_type=F32).astype(BF16)
    cols = out_ref.shape[2]
    for i in range(both.shape[1] // cols):
        out_ref[i] = both[:, i * cols : (i + 1) * cols]
    wide = part_ref[...].astype(F32)
    moment_next = 0.95 * moment_ref[...] + 0.05 * wide * wide
    next_ref[...] = moment_next
    adam = wide / (jnp.sqrt(moment_next) + 1e-08)
    square = jnp.sum(jnp.sum(adam * adam, axis=0, keepdims=True), axis=1, keepdims=True)
    held_ref[step] = jnp.broadcast_to(square, held_ref.shape[1:])

    @pl.when(step == steps - 1)
    def _():
        count = held_ref.shape[0] // col_blocks
        values = []
        for c in range(col_blocks):
            total = held_ref[c * count]
            for i in range(1, count):
                total = total + held_ref[c * count + i]
            values += split3(total)
        lane = lax.broadcasted_iota(jnp.int32, sums_ref.shape, 1)
        out = jnp.zeros(sums_ref.shape, F32)
        for i, value in enumerate(values):
            out = jnp.where(lane == 3 + i, value, out)
        sums_ref[...] = out


def reverse_kernel(left_ref, out_ref, sems):
    copies = [
        pltpu.make_async_copy(left_ref.at[z], out_ref.at[ZH - 1 - z], sems.at[z])
        for z in range(ZH)
    ]
    for copy in copies:
        copy.start()
    for copy in copies:
        copy.wait()


def pack_kernel(core_ref, piece_ref, left_ref, out_ref):
    rows, cols = piece_ref.shape[1:]
    planes, sub, blk = left_ref.shape
    n = planes * sub
    half = blk // 2
    left = jnp.concatenate([left_ref[ZH - 1 - z].astype(F32) for z in range(ZH)], axis=0)
    left = left.astype(BF16)
    left = jnp.where(core_ref[0] == 0, left[:, :half], left[:, half:])
    for j in range(YY):
        out_ref[j, :rows] = piece_ref[j]
        for h in range(half // cols):
            out_ref[j, rows + h * n : rows + (h + 1) * n] = left[:, h * cols : (h + 1) * cols]


def product_kernel(strip_ref, left_ref, adam_ref, out_ref):
    rows, cols = strip_ref.shape[2:]
    sub = rows // XX
    n = ZH * sub
    steps = left_ref.shape[2] // n
    per = cols // (XX * rows)
    total = jnp.zeros((YY * n, cols), F32)
    for h in range(2 * steps):
        left = left_ref[h // steps, :, h % steps * n : (h % steps + 1) * n, :]
        tall = [strip_ref[i, h * per + j] for j in range(per) for i in range(XX)]
        tall = jnp.concatenate(tall, axis=0)
        total = total + jnp.dot(left.reshape(YY * n, cols), tall, preferred_element_type=F32)
    mixed = total.astype(BF16).astype(F32)
    square = jnp.sum(jnp.sum(mixed * mixed, axis=0, keepdims=True), axis=1, keepdims=True)
    sums = by_lane(split3(square), (1, LANES)) + adam_ref[...]
    sums = jnp.broadcast_to(sums, (sub, LANES))
    for y in range(YY):
        for z in range(ZH):
            m = (y * ZH + z) * sub
            piece = jnp.concatenate([mixed[m : m + sub], sums], axis=1)
            out_ref[z * YY + y] = piece.astype(BF16)


def update_kernel(col_blocks, back_ref, out_ref):
    peers, sub, both = back_ref.shape
    cols = both - LANES
    back = back_ref[...].astype(F32)
    sums = back[:, 0, cols:]
    lane = lax.broadcasted_iota(jnp.int32, (1, LANES), 1)
    every = jnp.sum(sums, axis=0, keepdims=True)
    share = peers // col_blocks
    for c in range(col_blocks):
        own = jnp.sum(sums[c * share : (c + 1) * share], axis=0, keepdims=True)
        mixed_sq = jnp.sum(jnp.where(lane < 3, own, 0.0), axis=1, keepdims=True)
        here = (lane >= 3 * (c + 1)) & (lane < 3 * (c + 2))
        adam_sq = jnp.sum(jnp.where(here, every, 0.0), axis=1, keepdims=True)
        factor = jnp.sqrt(adam_sq) / (jnp.sqrt(mixed_sq) + 1e-06)
        for j in range(c * YY // col_blocks, (c + 1) * YY // col_blocks):
            piece = back[j * XX : (j + 1) * XX, :, :cols].reshape(XX * sub, cols)
            out_ref[:, j * cols : (j + 1) * cols] = (piece * factor).astype(BF16)


def on_device(grad, second_moment, left_roots, right_roots):
    rows, width = grad.shape
    col_blocks, blk = right_roots.shape[:2]
    cols = width // YY
    sub = rows // XX
    backward = pl.pallas_call(
        reverse_kernel,
        out_shape=jax.ShapeDtypeStruct(left_roots.shape, BF16),
        in_specs=[pl.BlockSpec(memory_space=pl.ANY)],
        out_specs=pl.BlockSpec(memory_space=pl.ANY),
        scratch_shapes=[pltpu.SemaphoreType.DMA((ZH,))],
        name="reverse",
    )(left_roots)
    turned = [list(range(ZH))[::-1]]
    mine = lax.all_to_all(backward, "zh", 0, 0, axis_index_groups=turned, tiled=True)
    wide_cols = width // 4
    per_block = blk // wide_cols
    tile = lambda s: (0, s)
    pieces, moment_next, adam_sums = pl.pallas_call(
        functools.partial(right_kernel, col_blocks),
        grid=(4,),
        out_shape=(
            jax.ShapeDtypeStruct((YY, rows, cols), BF16),
            jax.ShapeDtypeStruct((rows, width), F32),
            jax.ShapeDtypeStruct((1, LANES), F32),
        ),
        in_specs=[
            pl.BlockSpec((rows, blk), lambda s: (0, s // per_block)),
            pl.BlockSpec((1, blk, wide_cols), lambda s: (s // per_block, 0, s % per_block)),
            pl.BlockSpec((rows, wide_cols), tile),
            pl.BlockSpec((rows, wide_cols), tile),
        ],
        out_specs=(
            pl.BlockSpec((YY // 4, rows, cols), lambda s: (s, 0, 0)),
            pl.BlockSpec((rows, wide_cols), tile),
            pl.BlockSpec((1, LANES), lambda s: (0, 0)),
        ),
        scratch_shapes=[pltpu.VMEM((4, 1, LANES), F32)],
        name="right",
        compiler_params=SMALL,
        cost_estimate=pl.CostEstimate(flops=2**27, bytes_accessed=2**22, transcendentals=2**16),
    )(grad, right_roots, grad, second_moment)
    send = pl.pallas_call(
        pack_kernel,
        out_shape=jax.ShapeDtypeStruct((YY, rows + ZH * sub * blk // (2 * cols), cols), BF16),
        in_specs=[SCALARS] + [WHOLE] * 2,
        out_specs=WHOLE,
        name="pack",
        compiler_params=SMALL,
        cost_estimate=pl.CostEstimate(flops=2**10, bytes_accessed=2**20, transcendentals=0),
    )(lax.axis_index("core")[None], pieces, mine)
    got = lax.all_to_all(send, "y", 0, 0, tiled=True)
    left = lax.all_gather(got[:, rows:], "core", axis=0)
    strip = jnp.broadcast_to(got[None, :, :rows], (XX, YY, rows, cols))
    strip = lax.all_to_all(strip, "x", 0, 0, tiled=True)
    ready = pl.pallas_call(
        product_kernel,
        out_shape=jax.ShapeDtypeStruct((PEERS, sub, cols + LANES), BF16),
        in_specs=[WHOLE] * 3,
        out_specs=WHOLE,
        name="product",
        compiler_params=SMALL,
        cost_estimate=pl.CostEstimate(flops=2**28, bytes_accessed=2**21, transcendentals=0),
    )(strip, left, adam_sums)
    back = lax.all_to_all(ready, PLANE, 0, 0, tiled=True)
    update = pl.pallas_call(
        functools.partial(update_kernel, col_blocks),
        out_shape=jax.ShapeDtypeStruct((rows, width), BF16),
        in_specs=[WHOLE],
        out_specs=WHOLE,
        name="update",
        compiler_params=SMALL,
        cost_estimate=pl.CostEstimate(flops=2**22, bytes_accessed=2**19, transcendentals=0),
    )(back)
    return (update, moment_next)


def solution(mesh):
    tensor = mesh.shape["tensor"]
    names = ("zh", "y", "x", "zl", "core")
    fine = Mesh(mesh.devices.reshape(ZH, YY, XX, tensor // 2, 2), names)
    dp, columns = ("zh", "y", "x"), ("zl", "core")
    return jax.shard_map(
        on_device,
        mesh=fine,
        in_specs=(
            P(dp, columns),
            P(dp, columns),
            P(None, dp, None),
            P(columns, None, None),
        ),
        out_specs=(P(dp, columns), P(dp, columns)),
        check_vma=False,
    )
```
